32 devices in a mesh: groups: 2 (over y), batch: 8 (over z, x), mp: 2 (over core).
Axes of the slice: x: 2, y: 2, z: 4, core: 2. Of those that a mesh axis runs over, the one named last changes fastest.
Arguments:
- tokens: bfloat16 [1024, 16384], P(('groups', 'batch')), parts along dimension 0, may hold values from -6 to 6
- gate_weight: bfloat16 [16384, 256], P('batch', 'mp'), may hold values from -0.046875 to 0.046875
- up_weight: bfloat16 [16384, 256], P('batch', 'mp'), may hold values from -0.046875 to 0.046875
- down_weight: bfloat16 [256, 16384], P('mp', 'batch'), may hold values from -0.5 to 0.5
Outputs:
- mixed: bfloat16 [1024, 16384], P(('groups', 'batch'), 'mp'), parts along dimension 0
The draws below stay inside these ranges and needn't reach their ends.
There are 2 independent parts, one for each index of `groups`. The reference program is written for one: setup_inputs(seed, part) draws one part's arguments, and reference() takes and returns one part's arrays. A program takes and returns all parts, laid end to end along the dimension named above; an argument that names none is the same for every part. Nothing has to cross between parts.
All inputs are finite; a program needn't handle non-finite values.
Results may differ from the reference program's by a relative error of at most 0.018.
Values may be sent and summed in bfloat16 or wider, within the bound.
A program may use at most 64 MiB of HBM per device.

```python
import jax
import jax.numpy as jnp
from jax import lax

D = 16384
HID_DEV = 128
TOKENS = 512
FF = 256
N_MP = 2


def strengthened(drawn, stream_key, source, target, shards_of, factor):
    def block_of(dim):
        return (jnp.arange(drawn.shape[dim]) // (drawn.shape[dim] // shards_of)).reshape((-1,) + (1,) * (drawn.ndim - 1 - dim))

    first = jax.random.permutation(stream_key, shards_of)[block_of(target)]
    other_side = (block_of(target) + shards_of // 2) % shards_of
    return jnp.where((block_of(source) == first) | (block_of(source) == other_side), factor * drawn, drawn)


def steps_of(stream_key, extent, shards, least, top_value):
    level, own = 1.0, jax.random.fold_in(stream_key, 6)
    for position, parts in shards:
        steps = jnp.exp(jax.random.uniform(jax.random.fold_in(own, position), (parts,), jnp.float32, least / len(shards), top_value / len(shards)))
        level = level * jnp.repeat(steps, extent[position] // parts).reshape([-1 if axis == position else 1 for axis in range(len(extent))])
    return level


def bell_draw(own_key, dims, spread, limit, split=(), held_as=jnp.bfloat16):
    drawn = spread * jax.random.normal(own_key, dims, jnp.float32)
    if split:
        drawn = drawn * steps_of(own_key, dims, split, -0.22, 0.18)
    return jnp.clip(drawn, -limit, limit).astype(held_as)


def bell_draw_with(own_key, extent, width, most, split, heavy, dtype=jnp.bfloat16):
    entries = width * jax.random.normal(own_key, extent, jnp.float32)
    if split:
        entries = entries * steps_of(own_key, extent, split, -0.22, 0.18)
    return jnp.clip(strengthened(entries, jax.random.fold_in(own_key, 3), *heavy), -most, most).astype(dtype)


def setup_inputs(seed: int = 0, part: int = 0) -> dict:
    key_list = jax.random.split(jax.random.key(seed), 5)
    part_keys = jax.random.split(jax.random.fold_in(key_list[4], part), 5)
    tokens = bell_draw(part_keys[0], (TOKENS, D), 1.0, 6.0, ((0, 8),))
    gate_weight = bell_draw(key_list[1], (D, FF), D ** -0.5, 0.046875, ((0, 8), (1, 2)))
    up_weight = bell_draw(key_list[2], (D, FF), D ** -0.5, 0.046875, ((0, 8), (1, 2)))
    down_weight = bell_draw_with(key_list[3], (FF, D), FF ** -0.5, 0.5, ((0, 2), (1, 8)), (0, 1, 8, 2.0))
    return dict(tokens=tokens, gate_weight=gate_weight, up_weight=up_weight, down_weight=down_weight)


def reference(tokens, gate_weight, up_weight, down_weight):
    gate = jnp.dot(tokens, gate_weight, preferred_element_type=jnp.float32)
    up = jnp.dot(tokens, up_weight, preferred_element_type=jnp.float32)
    hidden = (jax.nn.silu(gate) * up).astype(jnp.bfloat16)
    rows = hidden.shape[0]
    hidden_groups = jnp.transpose(hidden.reshape(rows, N_MP, HID_DEV), (1, 0, 2))
    down_groups = down_weight.reshape(N_MP, HID_DEV, down_weight.shape[1])

    def add_group(total, pair):
        partial_value = jnp.dot(pair[0], pair[1], preferred_element_type=jnp.float32).astype(jnp.bfloat16)
        partial_value = lax.optimization_barrier(partial_value)
        return total + partial_value.astype(jnp.float32), None

    start = jnp.zeros((rows, down_weight.shape[1]), jnp.float32)
    total, unused = lax.scan(add_group, start, (hidden_groups, down_groups))
    return total.astype(jnp.bfloat16)
```

```python
import functools

import jax
import jax.numpy as jnp
from jax import lax
from jax.experimental import pallas as pl
from jax.experimental.pallas import tpu as pltpu
from jax.sharding import PartitionSpec as P

MESH = pl.DeviceIdType.MESH


def gathered(tokens, gate_weight, up_weight, down_weight):
    gate_sum = jnp.dot(
        tokens,
        lax.all_gather(gate_weight, "batch", axis=0, tiled=True),
        preferred_element_type=jnp.float32,
    )
    up_sum = jnp.dot(
        tokens,
        lax.all_gather(up_weight, "batch", axis=0, tiled=True),
        preferred_element_type=jnp.float32,
    )
    hidden = (jax.nn.silu(gate_sum) * up_sum).astype(jnp.bfloat16)
    partial_value = jnp.dot(
        hidden,
        lax.all_gather(down_weight, "batch", axis=1, tiled=True),
        preferred_element_type=jnp.float32,
    )
    return lax.psum_scatter(
        partial_value.astype(jnp.bfloat16), "mp", scatter_dimension=1, tiled=True
    )


def kernel(
    nb, tok, gate_w, up_w, down_w, out,
    wbuf, tbuf, dbuf, pbuf, rbuf, hsrc, hbuf, obuf,
    loc_sem, wsend, wrecv, tsend, trecv, psend, precv, hsend, hrecv, osend, orecv,
):
    b, m = lax.axis_index("batch"), lax.axis_index("mp")
    other = 1 - m
    rows, width = tok.shape
    half = rows // 2
    depth, hid = gate_w.shape
    cols = down_w.shape[1]
    per_owner = nb // 2
    owner, place = b // per_owner, b % per_owner

    def at(index, size):
        return pl.ds(pl.multiple_of(index * size, size), size)

    def peer(i):
        return lax.rem(b + i, nb)

    def remote(src, dst, send, recv, chip, core):
        return pltpu.make_async_remote_copy(
            src_ref=src, dst_ref=dst, send_sem=send, recv_sem=recv,
            device_id={"batch": chip, "mp": core}, device_id_type=MESH,
        )

    def swap(k):
        src, dst = [
            (gate_w, wbuf.at[:, at(m, hid)]),
            (up_w, wbuf.at[:, at(2 + m, hid)]),
            (down_w, dbuf.at[at(m, hid), :]),
        ][k]
        return src, dst

    def token_copy(i):
        chip = peer(i)
        return remote(
            tok.at[at(m, half), at(chip, depth)], tbuf.at[at(b, half), :],
            tsend.at[chip], trecv.at[b], chip, m,
        )

    def partial_copy(chip):
        return remote(pbuf.at[chip], rbuf.at[b], psend.at[chip], precv.at[b], chip, m)

    def hidden_copy(i):
        chip = peer(i)
        return remote(hsrc, hbuf.at[at(b, half), :], hsend.at[chip], hrecv.at[b], chip, m)

    slot = place * 2 + m

    def out_dst():
        return out.at[at(m, half), at(place, cols)]

    def out_copy(chip):
        return remote(
            obuf.at[at(chip, half), :], out_dst(), osend.at[chip], orecv.at[slot], chip, owner
        )

    local = [pltpu.make_async_copy(*swap(k), loc_sem.at[k]) for k in range(3)]
    local.append(
        pltpu.make_async_copy(
            tok.at[at(m, half), at(b, depth)], tbuf.at[at(b, half), :], loc_sem.at[3]
        )
    )
    for copy in local:
        copy.start()

    barrier = pltpu.get_barrier_semaphore()
    for i in range(nb):
        for j in range(2):
            if i or j:
                pl.semaphore_signal(
                    barrier, inc=1,
                    device_id={"batch": peer(i), "mp": lax.rem(m + j, 2)},
                    device_id_type=MESH,
                )
    pl.semaphore_wait(barrier, 2 * nb - 1)

    for i in range(1, nb):
        token_copy(i).start()
    swaps = []
    for k in range(3):
        src, dst = swap(k)
        swaps.append(remote(src, dst, wsend.at[k], wrecv.at[k], b, other))
        swaps[-1].start()
    for copy in local:
        copy.wait()
    for k in range(2):
        swaps[k].wait_recv()

    z, x = b // 2, b % 2

    def first(step, carry):
        pair = lax.rem(z + step, nb // 2)
        for j in range(2):
            chip = pair * 2 + j

            @pl.when(chip != b)
            def _():
                remote(
                    tok.at[at(m, half), at(chip, depth)], tbuf.at[at(chip, half), :],
                    tsend.at[chip], trecv.at[chip], chip, m,
                ).wait_recv()

        sums = jnp.dot(
            tbuf[at(pair, rows), :], wbuf[...], preferred_element_type=jnp.float32
        ).astype(jnp.bfloat16)
        for j in range(2):
            chip = pair * 2 + j
            pbuf[chip] = sums[j * half : (j + 1) * half]

            @pl.when(chip != b)
            def _():
                partial_copy(chip).start()

        return carry

    lax.fori_loop(0, nb // 2, first, 0)

    total = pbuf[b].astype(jnp.float32)
    for i in range(1, nb):
        chip = peer(i)
        remote(
            pbuf.at[chip], rbuf.at[chip], psend.at[chip], precv.at[chip], chip, m
        ).wait_recv()
        total += rbuf[chip].astype(jnp.float32)
    gate, up = total[:, : 2 * hid], total[:, 2 * hid :]
    hidden = (gate / (1.0 + jnp.exp(-gate)) * up).astype(jnp.bfloat16)
    hsrc[...] = hidden
    for i in range(1, nb):
        hidden_copy(i).start()
    hbuf[at(b, half), :] = hidden
    swaps[2].wait_recv()

    def second(step, carry):
        pair = lax.rem(z + step, nb // 2)
        for j in range(2):
            chip = pair * 2 + j

            @pl.when(chip != b)
            def _():
                remote(
                    hsrc, hbuf.at[at(chip, half), :], hsend.at[chip], hrecv.at[chip], chip, m
                ).wait_recv()

        obuf[at(pair, rows), :] = jnp.dot(
            hbuf[at(pair, rows), :], dbuf[...], preferred_element_type=jnp.float32
        ).astype(jnp.bfloat16)
        for j in range(2):
            chip = pair * 2 + j
            here = jnp.logical_and(chip == b, owner == m)

            @pl.when(jnp.logical_not(here))
            def _():
                out_copy(chip).start()

            @pl.when(here)
            def _():
                pltpu.make_async_copy(
                    obuf.at[at(chip, half), :], out_dst(), orecv.at[slot]
                ).start()

        return carry

    lax.fori_loop(0, nb // 2, second, 0)

    for i in range(1, nb):
        token_copy(i).wait_send()
        partial_copy(peer(i)).wait_send()
        hidden_copy(i).wait_send()
        out_copy(peer(i)).wait_send()
    for copy in swaps:
        copy.wait_send()

    @pl.when(owner != m)
    def _():
        out_copy(b).wait_send()

    for k in range(per_owner):
        for j in range(2):
            pltpu.make_async_copy(
                obuf.at[pl.ds(0, half), :],
                out.at[pl.ds(j * half, half), pl.ds(k * cols, cols)],
                orecv.at[k * 2 + j],
            ).wait()


def exchanged(nb, tokens, gate_weight, up_weight, down_weight):
    rows, width = tokens.shape
    half = rows // 2
    depth, hid = gate_weight.shape
    cols = down_weight.shape[1]
    bf16 = jnp.bfloat16
    sems = [4, 3, 3] + [nb] * 8
    return pl.pallas_call(
        functools.partial(kernel, nb),
        out_shape=jax.ShapeDtypeStruct((rows, width // 2), bf16),
        in_specs=[pl.BlockSpec(memory_space=pl.ANY)] * 4,
        out_specs=pl.BlockSpec(memory_space=pl.ANY),
        scratch_shapes=[
            pltpu.VMEM((depth, 4 * hid), bf16),
            pltpu.VMEM((nb * half, depth), bf16),
            pltpu.VMEM((2 * hid, cols), bf16),
            pltpu.VMEM((nb, half, 4 * hid), bf16),
            pltpu.VMEM((nb, half, 4 * hid), bf16),
            pltpu.VMEM((half, 2 * hid), bf16),
            pltpu.VMEM((nb * half, 2 * hid), bf16),
            pltpu.VMEM((nb * half, cols), bf16),
        ] + [pltpu.SemaphoreType.DMA((n,)) for n in sems],
        compiler_params=pltpu.CompilerParams(
            collective_id=0, has_side_effects=True, vmem_limit_bytes=40 * 2**20
        ),
    )(tokens, gate_weight, up_weight, down_weight)


def solution(mesh):
    nb = mesh.shape["batch"]
    small = mesh.shape["mp"] == 2 and nb % 2 == 0
    return jax.shard_map(
        functools.partial(exchanged, nb) if small else gathered,
        mesh=mesh,
        in_specs=(
            P(("groups", "batch"), None),
            P("batch", "mp"),
            P("batch", "mp"),
            P("mp", "batch"),
        ),
        out_specs=P(("groups", "batch"), "mp"),
        check_vma=False,
    )
```

```python
import functools

import jax
import jax.numpy as jnp
from jax import lax
from jax.experimental import pallas as pl
from jax.experimental.pallas import tpu as pltpu
from jax.sharding import PartitionSpec as P

MESH = pl.DeviceIdType.MESH


def gathered(tokens, gate_weight, up_weight, down_weight):
    gate_sum = jnp.dot(
        tokens,
        lax.all_gather(gate_weight, "batch", axis=0, tiled=True),
        preferred_element_type=jnp.float32,
    )
    up_sum = jnp.dot(
        tokens,
        lax.all_gather(up_weight, "batch", axis=0, tiled=True),
        preferred_element_type=jnp.float32,
    )
    hidden = (jax.nn.silu(gate_sum) * up_sum).astype(jnp.bfloat16)
    partial_value = jnp.dot(
        hidden,
        lax.all_gather(down_weight, "batch", axis=1, tiled=True),
        preferred_element_type=jnp.float32,
    )
    return lax.psum_scatter(
        partial_value.astype(jnp.bfloat16), "mp", scatter_dimension=1, tiled=True
    )


def kernel(
    nb, parts, tok, gate_w, up_w, down_w, out,
    wbuf, tbuf, dbuf, pbuf, rbuf, hsrc, hbuf, obuf,
    loc_sem, wsend, wrecv, tsend, trecv, psend, precv, hsend, hrecv, osend, orecv,
):
    b, m = lax.axis_index("batch"), lax.axis_index("mp")
    other = 1 - m
    rows = tok.shape[0]
    half = rows // 2
    size = half // parts
    depth, hid = gate_w.shape
    cols = down_w.shape[1]
    nz = nb // 2
    z, x = b // 2, b % 2
    across = 2 * z + 1 - x
    per_owner = nz // 2
    owner, place = z // per_owner, z % per_owner

    def at(index, extent):
        return pl.ds(pl.multiple_of(index * extent, extent), extent)

    def remote(src, dst, send, recv, chip, core):
        return pltpu.make_async_remote_copy(
            src_ref=src, dst_ref=dst, send_sem=send, recv_sem=recv,
            device_id={"batch": chip, "mp": core}, device_id_type=MESH,
        )

    def mine(c):
        return pl.ds(pl.multiple_of(m * half + c * size, size), size)

    def token_copy(c, chip, source):
        return remote(
            tok.at[mine(c), at(chip, depth)], tbuf.at[at(c * nb + source, size), :],
            tsend.at[c * nb + chip], trecv.at[c * nb + source], chip, m,
        )

    def partial_copy(c, chip, source):
        return remote(
            pbuf.at[c * nb + chip], rbuf.at[c * nb + source],
            psend.at[c * nb + chip], precv.at[c * nb + source], chip, m,
        )

    def hidden_copy(c, zone, source):
        return remote(
            hsrc.at[c], hbuf.at[at(c * nz + source, size), :],
            hsend.at[c * nz + zone], hrecv.at[c * nz + source], 2 * zone + x, m,
        )

    def slot(c):
        return (c * per_owner + place) * 2 + m

    def out_dst(c):
        return out.at[mine(c), at(place, 2 * cols)]

    def out_src(c, zone):
        return obuf.at[at(c * nz + zone, size), :]

    def out_copy(c, zone):
        return remote(
            out_src(c, zone), out_dst(c), osend.at[c * nz + zone], orecv.at[slot(c)],
            2 * zone + x, owner,
        )

    own_down = dbuf.at[at(m, hid), at(x, cols)]
    swapped = [
        (gate_w, wbuf.at[:, at(m, hid)]),
        (up_w, wbuf.at[:, at(2 + m, hid)]),
        (down_w, own_down),
    ]
    local = [pltpu.make_async_copy(*pair, loc_sem.at[k]) for k, pair in enumerate(swapped)]
    for c in range(parts):
        local.append(
            pltpu.make_async_copy(
                tok.at[mine(c), at(b, depth)], tbuf.at[at(c * nb + b, size), :],
                loc_sem.at[3 + c],
            )
        )
    for copy in local:
        copy.start()

    barrier = pltpu.get_barrier_semaphore()
    for i in range(nb):
        for j in range(2):
            if i or j:
                pl.semaphore_signal(
                    barrier, inc=1,
                    device_id={"batch": lax.rem(b + i, nb), "mp": lax.rem(m + j, 2)},
                    device_id_type=MESH,
                )
    pl.semaphore_wait(barrier, 2 * nb - 1)

    swaps = [
        remote(src, dst, wsend.at[k], wrecv.at[k], b, other)
        for k, (src, dst) in enumerate(swapped)
    ]
    over = remote(down_w, own_down, wsend.at[3], wrecv.at[3], across, m)
    got = dbuf.at[at(m, hid), at(1 - x, cols)]
    onward = remote(got, got, wsend.at[4], wrecv.at[4], b, other)

    for i in range(1, nb):
        token_copy(0, lax.rem(b + i, nb), b).start()
    swaps[0].start()
    swaps[1].start()
    for c in range(1, parts):
        for i in range(1, nb):
            token_copy(c, lax.rem(b + i, nb), b).start()
    swaps[2].start()
    over.start()
    for copy in local:
        copy.wait()
    swaps[0].wait_recv()
    swaps[1].wait_recv()

    def first(c):
        def pair_of_chips(step, carry):
            zone = lax.rem(z + step, nz)
            for j in range(2):
                chip = zone * 2 + j

                @pl.when(chip != b)
                def _():
                    token_copy(c, chip, chip).wait_recv()

            sums = jnp.dot(
                tbuf[at(c * nz + zone, 2 * size), :], wbuf[...],
                preferred_element_type=jnp.float32,
            ).astype(jnp.bfloat16)
            for j in range(2):
                chip = zone * 2 + j
                pbuf[c * nb + chip] = sums[j * size : (j + 1) * size]

                @pl.when(chip != b)
                def _():
                    partial_copy(c, chip, b).start()

            return carry

        lax.fori_loop(0, nz, pair_of_chips, 0)

    def reduce(c):
        total = pbuf[c * nb + b].astype(jnp.float32)
        for i in range(1, nb):
            chip = lax.rem(b + i, nb)
            partial_copy(c, chip, chip).wait_recv()
            total += rbuf[c * nb + chip].astype(jnp.float32)
        gate, up = total[:, : 2 * hid], total[:, 2 * hid :]
        hidden = (gate / (1.0 + jnp.exp(-gate)) * up).astype(jnp.bfloat16)
        hsrc[c] = hidden
        for i in range(1, nz):
            hidden_copy(c, lax.rem(z + i, nz), z).start()
        hbuf[at(c * nz + z, size), :] = hidden

    def second(c):
        for i in range(1, nz):
            zone = lax.rem(z + i, nz)
            hidden_copy(c, zone, zone).wait_recv()
        obuf[c * nz * size : (c + 1) * nz * size, :] = jnp.dot(
            hbuf[c * nz * size : (c + 1) * nz * size, :], dbuf[...],
            preferred_element_type=jnp.float32,
        ).astype(jnp.bfloat16)
        for i in range(1, nz):
            out_copy(c, lax.rem(z + i, nz)).start()

        @pl.when(owner != m)
        def _():
            out_copy(c, z).start()

        @pl.when(owner == m)
        def _():
            pltpu.make_async_copy(out_src(c, z), out_dst(c), orecv.at[slot(c)]).start()

    first(0)
    over_in = remote(got, got, wsend.at[3], wrecv.at[3], across, m)
    over_in.wait_recv()
    onward.start()
    for c in range(parts):
        reduce(c)
        if c + 1 < parts:
            first(c + 1)
        if c == 0:
            swaps[2].wait_recv()
            onward.wait_recv()
        second(c)

    for c in range(parts):
        for i in range(1, nb):
            chip = lax.rem(b + i, nb)
            token_copy(c, chip, b).wait_send()
            partial_copy(c, chip, b).wait_send()
        for i in range(1, nz):
            zone = lax.rem(z + i, nz)
            hidden_copy(c, zone, z).wait_send()
            out_copy(c, zone).wait_send()

        @pl.when(owner != m)
        def _():
            out_copy(c, z).wait_send()

    for copy in swaps + [over, onward]:
        copy.wait_send()

    for c in range(parts):
        for k in range(per_owner):
            for j in range(2):
                pltpu.make_async_copy(
                    obuf.at[pl.ds(0, size), :],
                    out.at[pl.ds(j * half + c * size, size), pl.ds(k * 2 * cols, 2 * cols)],
                    orecv.at[(c * per_owner + k) * 2 + j],
                ).wait()


def exchanged(nb, tokens, gate_weight, up_weight, down_weight):
    rows, width = tokens.shape
    half = rows // 2
    parts = 2
    size = half // parts
    depth, hid = gate_weight.shape
    cols = down_weight.shape[1]
    nz = nb // 2
    bf16 = jnp.bfloat16
    sems = [3 + parts, 5, 5] + [parts * nb] * 4 + [parts * nz] * 4
    return pl.pallas_call(
        functools.partial(kernel, nb, parts),
        out_shape=jax.ShapeDtypeStruct((rows, width // 2), bf16),
        in_specs=[pl.BlockSpec(memory_space=pltpu.HBM)] * 4,
        out_specs=pl.BlockSpec(memory_space=pltpu.HBM),
        scratch_shapes=[
            pltpu.VMEM((depth, 4 * hid), bf16),
            pltpu.VMEM((nb * half, depth), bf16),
            pltpu.VMEM((2 * hid, 2 * cols), bf16),
            pltpu.VMEM((parts * nb, size, 4 * hid), bf16),
            pltpu.VMEM((parts * nb, size, 4 * hid), bf16),
            pltpu.VMEM((parts, size, 2 * hid), bf16),
            pltpu.VMEM((nz * half, 2 * hid), bf16),
            pltpu.VMEM((nz * half, 2 * cols), bf16),
        ] + [pltpu.SemaphoreType.DMA((n,)) for n in sems],
        compiler_params=pltpu.CompilerParams(
            collective_id=0, has_side_effects=True, vmem_limit_bytes=40 * 2**20
        ),
    )(tokens, gate_weight, up_weight, down_weight)


def solution(mesh):
    nb = mesh.shape["batch"]
    small = mesh.shape["mp"] == 2 and nb % 4 == 0
    return jax.shard_map(
        functools.partial(exchanged, nb) if small else gathered,
        mesh=mesh,
        in_specs=(
            P(("groups", "batch"), None),
            P("batch", "mp"),
            P("batch", "mp"),
            P("mp", "batch"),
        ),
        out_specs=P(("groups", "batch"), "mp"),
        check_vma=False,
    )
```

```python
import functools

import jax
import jax.numpy as jnp
from jax import lax
from jax.experimental import pallas as pl
from jax.experimental.pallas import tpu as pltpu
from jax.sharding import PartitionSpec as P

MESH = pl.DeviceIdType.MESH


def gathered(tokens, gate_weight, up_weight, down_weight):
    gate_sum = jnp.dot(
        tokens,
        lax.all_gather(gate_weight, "batch", axis=0, tiled=True),
        preferred_element_type=jnp.float32,
    )
    up_sum = jnp.dot(
        tokens,
        lax.all_gather(up_weight, "batch", axis=0, tiled=True),
        preferred_element_type=jnp.float32,
    )
    hidden = (jax.nn.silu(gate_sum) * up_sum).astype(jnp.bfloat16)
    partial_value = jnp.dot(
        hidden,
        lax.all_gather(down_weight, "batch", axis=1, tiled=True),
        preferred_element_type=jnp.float32,
    )
    return lax.psum_scatter(
        partial_value.astype(jnp.bfloat16), "mp", scatter_dimension=1, tiled=True
    )


def kernel(
    nb, parts, tok, gate_w, up_w, down_w, out,
    wbuf, tbuf, dbuf, pbuf, rbuf, hsrc, hbuf, obuf,
    loc_sem, wsend, wrecv, tsend, trecv, psend, precv, hsend, hrecv, osend, orecv,
):
    b, m = lax.axis_index("batch"), lax.axis_index("mp")
    other = 1 - m
    rows = tok.shape[0]
    half = rows // 2
    size = half // parts
    depth, hid = gate_w.shape
    cols = down_w.shape[1]
    nz = nb // 2
    z, x = b // 2, b % 2
    across = 2 * z + 1 - x
    per_owner = nz // 2
    owner, place = z // per_owner, z % per_owner

    def at(index, extent):
        return pl.ds(pl.multiple_of(index * extent, extent), extent)

    def remote(src, dst, send, recv, chip, core):
        return pltpu.make_async_remote_copy(
            src_ref=src, dst_ref=dst, send_sem=send, recv_sem=recv,
            device_id={"batch": chip, "mp": core}, device_id_type=MESH,
        )

    def mine(c):
        return pl.ds(pl.multiple_of(m * half + c * size, size), size)

    def token_copy(c, chip, source):
        return remote(
            tok.at[mine(c), at(chip, depth)], tbuf.at[at(c * nb + source, size), :],
            tsend.at[c * nb + chip], trecv.at[c * nb + source], chip, m,
        )

    def partial_copy(c, chip, source):
        return remote(
            pbuf.at[c * nb + chip], rbuf.at[c * nb + source],
            psend.at[c * nb + chip], precv.at[c * nb + source], chip, m,
        )

    def hidden_copy(c, zone, source):
        return remote(
            hsrc.at[c], hbuf.at[at(c * nz + source, size), :],
            hsend.at[c * nz + zone], hrecv.at[c * nz + source], 2 * zone + x, m,
        )

    def slot(c):
        return (c * per_owner + place) * 2 + m

    def out_dst(c):
        return out.at[mine(c), at(place, 2 * cols)]

    def out_src(c, zone):
        return obuf.at[at(c * nz + zone, size), :]

    def out_copy(c, zone):
        return remote(
            out_src(c, zone), out_dst(c), osend.at[c * nz + zone], orecv.at[slot(c)],
            2 * zone + x, owner,
        )

    own_down = dbuf.at[at(m, hid), at(x, cols)]
    swapped = [
        (gate_w, wbuf.at[:, at(m, hid)]),
        (up_w, wbuf.at[:, at(2 + m, hid)]),
        (down_w, own_down),
    ]
    local = [pltpu.make_async_copy(*pair, loc_sem.at[k]) for k, pair in enumerate(swapped)]
    for c in range(parts):
        local.append(
            pltpu.make_async_copy(
                tok.at[mine(c), at(b, depth)], tbuf.at[at(c * nb + b, size), :],
                loc_sem.at[3 + c],
            )
        )
    for copy in local:
        copy.start()

    barrier = pltpu.get_barrier_semaphore()
    for i in range(nb):
        for j in range(2):
            if i or j:
                pl.semaphore_signal(
                    barrier, inc=1,
                    device_id={"batch": lax.rem(b + i, nb), "mp": lax.rem(m + j, 2)},
                    device_id_type=MESH,
                )
    pl.semaphore_wait(barrier, 2 * nb - 1)

    swaps = [
        remote(src, dst, wsend.at[k], wrecv.at[k], b, other)
        for k, (src, dst) in enumerate(swapped)
    ]
    over = remote(down_w, own_down, wsend.at[3], wrecv.at[3], across, m)
    got = dbuf.at[at(m, hid), at(1 - x, cols)]
    onward = remote(got, got, wsend.at[4], wrecv.at[4], b, other)

    for i in range(1, nb):
        token_copy(0, lax.rem(b + i, nb), b).start()
    swaps[0].start()
    swaps[1].start()
    for c in range(1, parts):
        for i in range(1, nb):
            token_copy(c, lax.rem(b + i, nb), b).start()
    swaps[2].start()
    over.start()
    for copy in local:
        copy.wait()
    swaps[0].wait_recv()
    swaps[1].wait_recv()

    def first(c):
        def pair_of_chips(step, carry):
            zone = lax.rem(z + nz - step, nz)
            for j in range(2):
                chip = zone * 2 + j

                @pl.when(chip != b)
                def _():
                    token_copy(c, chip, chip).wait_recv()

            sums = jnp.dot(
                tbuf[at(c * nz + zone, 2 * size), :], wbuf[...],
                preferred_element_type=jnp.float32,
            ).astype(jnp.bfloat16)
            for j in range(2):
                chip = zone * 2 + j
                pbuf[c * nb + chip] = sums[j * size : (j + 1) * size]

                @pl.when(chip != b)
                def _():
                    partial_copy(c, chip, b).start()

            return carry

        lax.fori_loop(0, nz, pair_of_chips, 0)

    def reduce(c):
        total = pbuf[c * nb + b].astype(jnp.float32)
        for i in range(1, nb):
            chip = lax.rem(b + nb - i, nb)
            partial_copy(c, chip, chip).wait_recv()
            total += rbuf[c * nb + chip].astype(jnp.float32)
        gate, up = total[:, : 2 * hid], total[:, 2 * hid :]
        hidden = (gate / (1.0 + jnp.exp(-gate)) * up).astype(jnp.bfloat16)
        hsrc[c] = hidden
        for i in range(1, nz):
            hidden_copy(c, lax.rem(z + i, nz), z).start()
        hbuf[at(c * nz + z, size), :] = hidden

    def second(c):
        for i in range(1, nz):
            zone = lax.rem(z + i, nz)
            hidden_copy(c, zone, zone).wait_recv()
        obuf[c * nz * size : (c + 1) * nz * size, :] = jnp.dot(
            hbuf[c * nz * size : (c + 1) * nz * size, :], dbuf[...],
            preferred_element_type=jnp.float32,
        ).astype(jnp.bfloat16)
        for i in range(1, nz):
            out_copy(c, lax.rem(z + i, nz)).start()

        @pl.when(owner != m)
        def _():
            out_copy(c, z).start()

        @pl.when(owner == m)
        def _():
            pltpu.make_async_copy(out_src(c, z), out_dst(c), orecv.at[slot(c)]).start()

    first(0)
    over_in = remote(got, got, wsend.at[3], wrecv.at[3], across, m)
    over_in.wait_recv()
    onward.start()
    for c in range(1, parts):
        first(c)
    swaps[2].wait_recv()
    onward.wait_recv()
    for c in range(parts):
        reduce(c)
        second(c)

    for c in range(parts):
        for i in range(1, nb):
            chip = lax.rem(b + i, nb)
            token_copy(c, chip, b).wait_send()
            partial_copy(c, chip, b).wait_send()
        for i in range(1, nz):
            zone = lax.rem(z + i, nz)
            hidden_copy(c, zone, z).wait_send()
            out_copy(c, zone).wait_send()

        @pl.when(owner != m)
        def _():
            out_copy(c, z).wait_send()

    for copy in swaps + [over, onward]:
        copy.wait_send()

    for c in range(parts):
        for k in range(per_owner):
            for j in range(2):
                pltpu.make_async_copy(
                    obuf.at[pl.ds(0, size), :],
                    out.at[pl.ds(j * half + c * size, size), pl.ds(k * 2 * cols, 2 * cols)],
                    orecv.at[(c * per_owner + k) * 2 + j],
                ).wait()


def exchanged(nb, tokens, gate_weight, up_weight, down_weight):
    rows, width = tokens.shape
    half = rows // 2
    parts = 2
    size = half // parts
    depth, hid = gate_weight.shape
    cols = down_weight.shape[1]
    nz = nb // 2
    bf16 = jnp.bfloat16
    sems = [3 + parts, 5, 5] + [parts * nb] * 4 + [parts * nz] * 4
    return pl.pallas_call(
        functools.partial(kernel, nb, parts),
        out_shape=jax.ShapeDtypeStruct((rows, width // 2), bf16),
        in_specs=[pl.BlockSpec(memory_space=pltpu.HBM)] * 4,
        out_specs=pl.BlockSpec(memory_space=pltpu.HBM),
        scratch_shapes=[
            pltpu.VMEM((depth, 4 * hid), bf16),
            pltpu.VMEM((nb * half, depth), bf16),
            pltpu.VMEM((2 * hid, 2 * cols), bf16),
            pltpu.VMEM((parts * nb, size, 4 * hid), bf16),
            pltpu.VMEM((parts * nb, size, 4 * hid), bf16),
            pltpu.VMEM((parts, size, 2 * hid), bf16),
            pltpu.VMEM((nz * half, 2 * hid), bf16),
            pltpu.VMEM((nz * half, 2 * cols), bf16),
        ] + [pltpu.SemaphoreType.DMA((n,)) for n in sems],
        compiler_params=pltpu.CompilerParams(
            collective_id=0, has_side_effects=True, vmem_limit_bytes=60 * 2**20
        ),
    )(tokens, gate_weight, up_weight, down_weight)


def solution(mesh):
    nb = mesh.shape["batch"]
    small = mesh.shape["mp"] == 2 and nb % 4 == 0
    return jax.shard_map(
        functools.partial(exchanged, nb) if small else gathered,
        mesh=mesh,
        in_specs=(
            P(("groups", "batch"), None),
            P("batch", "mp"),
            P("batch", "mp"),
            P("mp", "batch"),
        ),
        out_specs=P(("groups", "batch"), "mp"),
        check_vma=False,
    )
```

```python
import functools

import jax
import jax.numpy as jnp
from jax import lax
from jax.experimental import pallas as pl
from jax.experimental.pallas import tpu as pltpu
from jax.sharding import PartitionSpec as P

MESH = pl.DeviceIdType.MESH


def gathered(tokens, gate_weight, up_weight, down_weight):
    gate_sum = jnp.dot(
        tokens,
        lax.all_gather(gate_weight, "batch", axis=0, tiled=True),
        preferred_element_type=jnp.float32,
    )
    up_sum = jnp.dot(
        tokens,
        lax.all_gather(up_weight, "batch", axis=0, tiled=True),
        preferred_element_type=jnp.float32,
    )
    hidden = (jax.nn.silu(gate_sum) * up_sum).astype(jnp.bfloat16)
    partial_value = jnp.dot(
        hidden,
        lax.all_gather(down_weight, "batch", axis=1, tiled=True),
        preferred_element_type=jnp.float32,
    )
    return lax.psum_scatter(
        partial_value.astype(jnp.bfloat16), "mp", scatter_dimension=1, tiled=True
    )


def kernel(
    nb, parts, tok, gate_w, up_w, down_w, out,
    wbuf, tbuf, dbuf, pbuf, rbuf, hsrc, hbuf, obuf,
    loc_sem, wsend, wrecv, tsend, trecv, psend, precv, hsend, hrecv, osend, orecv,
):
    b, m = lax.axis_index("batch"), lax.axis_index("mp")
    other = 1 - m
    rows = tok.shape[0]
    half = rows // 2
    size = half // parts
    depth, hid = gate_w.shape
    cols = down_w.shape[1]
    nz = nb // 2
    z, x = b // 2, b % 2
    across = 2 * z + 1 - x
    per_owner = nz // 2
    owner, place = z // per_owner, z % per_owner

    def at(index, extent):
        return pl.ds(pl.multiple_of(index * extent, extent), extent)

    def remote(src, dst, send, recv, chip, core):
        return pltpu.make_async_remote_copy(
            src_ref=src, dst_ref=dst, send_sem=send, recv_sem=recv,
            device_id={"batch": chip, "mp": core}, device_id_type=MESH,
        )

    def mine(c):
        return pl.ds(pl.multiple_of(m * half + c * size, size), size)

    def token_copy(c, chip, source):
        return remote(
            tok.at[mine(c), at(chip, depth)], tbuf.at[at(c * nb + source, size), :],
            tsend.at[c * nb + chip], trecv.at[c * nb + source], chip, m,
        )

    def partial_copy(c, chip, source):
        return remote(
            pbuf.at[c * nb + chip], rbuf.at[c * nb + source],
            psend.at[c * nb + chip], precv.at[c * nb + source], chip, m,
        )

    def hidden_copy(c, zone, source):
        return remote(
            hsrc.at[c], hbuf.at[at(c * nz + source, size), :],
            hsend.at[c * nz + zone], hrecv.at[c * nz + source], 2 * zone + x, m,
        )

    def slot(c):
        return (c * per_owner + place) * 2 + m

    def out_dst(c):
        return out.at[mine(c), at(place, 2 * cols)]

    def out_src(c, zone):
        return obuf.at[at(c * nz + zone, size), :]

    def out_copy(c, zone):
        return remote(
            out_src(c, zone), out_dst(c), osend.at[c * nz + zone], orecv.at[slot(c)],
            2 * zone + x, owner,
        )

    own_down = dbuf.at[at(m, hid), at(x, cols)]
    swapped = [
        (gate_w, wbuf.at[:, at(m, hid)]),
        (up_w, wbuf.at[:, at(2 + m, hid)]),
        (down_w, own_down),
    ]
    local = [pltpu.make_async_copy(*pair, loc_sem.at[k]) for k, pair in enumerate(swapped)]
    for c in range(parts):
        local.append(
            pltpu.make_async_copy(
                tok.at[mine(c), at(b, depth)], tbuf.at[at(c * nb + b, size), :],
                loc_sem.at[3 + c],
            )
        )
    for copy in local:
        copy.start()

    barrier = pltpu.get_barrier_semaphore()
    for i in range(nb):
        for j in range(2):
            if i or j:
                pl.semaphore_signal(
                    barrier, inc=1,
                    device_id={"batch": lax.rem(b + i, nb), "mp": lax.rem(m + j, 2)},
                    device_id_type=MESH,
                )
    pl.semaphore_wait(barrier, 2 * nb - 1)

    swaps = [
        remote(src, dst, wsend.at[k], wrecv.at[k], b, other)
        for k, (src, dst) in enumerate(swapped)
    ]
    over = remote(down_w, own_down, wsend.at[3], wrecv.at[3], across, m)
    got = dbuf.at[at(m, hid), at(1 - x, cols)]
    onward = remote(got, got, wsend.at[4], wrecv.at[4], b, other)

    for i in range(1, nb):
        token_copy(0, lax.rem(b + i, nb), b).start()
    swaps[0].start()
    swaps[1].start()
    for c in range(1, parts):
        for i in range(1, 4):
            token_copy(c, lax.rem(b + i, nb), b).start()
    swaps[2].start()
    over.start()
    for copy in local:
        copy.wait()
    swaps[0].wait_recv()
    swaps[1].wait_recv()

    def first(c, low=0, high=nb // 2):
        def pair_of_chips(step, carry):
            zone = lax.rem(z + nz - step, nz)
            for j in range(2):
                chip = zone * 2 + j

                @pl.when(chip != b)
                def _():
                    token_copy(c, chip, chip).wait_recv()

            sums = jnp.dot(
                tbuf[at(c * nz + zone, 2 * size), :], wbuf[...],
                preferred_element_type=jnp.float32,
            ).astype(jnp.bfloat16)
            for j in range(2):
                chip = zone * 2 + j
                pbuf[c * nb + chip] = sums[j * size : (j + 1) * size]

                @pl.when(chip != b)
                def _():
                    partial_copy(c, chip, b).start()

            return carry

        lax.fori_loop(low, high, pair_of_chips, 0)

    def reduce(c):
        total = pbuf[c * nb + b].astype(jnp.float32)
        for i in range(1, nb):
            chip = lax.rem(b + nb - i, nb)
            partial_copy(c, chip, chip).wait_recv()
            total += rbuf[c * nb + chip].astype(jnp.float32)
        gate, up = total[:, : 2 * hid], total[:, 2 * hid :]
        hidden = (gate / (1.0 + jnp.exp(-gate)) * up).astype(jnp.bfloat16)
        hsrc[c] = hidden
        for i in range(1, nz):
            hidden_copy(c, lax.rem(z + i, nz), z).start()
        hbuf[at(c * nz + z, size), :] = hidden

    def second(c):
        for i in range(1, nz):
            zone = lax.rem(z + i, nz)
            hidden_copy(c, zone, zone).wait_recv()
        obuf[c * nz * size : (c + 1) * nz * size, :] = jnp.dot(
            hbuf[c * nz * size : (c + 1) * nz * size, :], dbuf[...],
            preferred_element_type=jnp.float32,
        ).astype(jnp.bfloat16)
        for i in range(1, nz):
            out_copy(c, lax.rem(z + i, nz)).start()

        @pl.when(owner != m)
        def _():
            out_copy(c, z).start()

        @pl.when(owner == m)
        def _():
            pltpu.make_async_copy(out_src(c, z), out_dst(c), orecv.at[slot(c)]).start()

    first(0)
    for c in range(1, parts):
        for i in range(4, nb):
            token_copy(c, lax.rem(b + i, nb), b).start()
    over_in = remote(got, got, wsend.at[3], wrecv.at[3], across, m)
    over_in.wait_recv()
    onward.start()
    first(1, 0, 1)
    reduce(0)
    first(1, 1, nz)
    swaps[2].wait_recv()
    onward.wait_recv()
    second(0)
    reduce(1)
    second(1)

    for c in range(parts):
        for i in range(1, nb):
            chip = lax.rem(b + i, nb)
            token_copy(c, chip, b).wait_send()
            partial_copy(c, chip, b).wait_send()
        for i in range(1, nz):
            zone = lax.rem(z + i, nz)
            hidden_copy(c, zone, z).wait_send()
            out_copy(c, zone).wait_send()

        @pl.when(owner != m)
        def _():
            out_copy(c, z).wait_send()

    for copy in swaps + [over, onward]:
        copy.wait_send()

    for c in range(parts):
        for k in range(per_owner):
            for j in range(2):
                pltpu.make_async_copy(
                    obuf.at[pl.ds(0, size), :],
                    out.at[pl.ds(j * half + c * size, size), pl.ds(k * 2 * cols, 2 * cols)],
                    orecv.at[(c * per_owner + k) * 2 + j],
                ).wait()


def exchanged(nb, tokens, gate_weight, up_weight, down_weight):
    rows, width = tokens.shape
    half = rows // 2
    parts = 2
    size = half // parts
    depth, hid = gate_weight.shape
    cols = down_weight.shape[1]
    nz = nb // 2
    bf16 = jnp.bfloat16
    sems = [3 + parts, 5, 5] + [parts * nb] * 4 + [parts * nz] * 4
    return pl.pallas_call(
        functools.partial(kernel, nb, parts),
        out_shape=jax.ShapeDtypeStruct((rows, width // 2), bf16),
        in_specs=[pl.BlockSpec(memory_space=pltpu.HBM)] * 4,
        out_specs=pl.BlockSpec(memory_space=pltpu.HBM),
        scratch_shapes=[
            pltpu.VMEM((depth, 4 * hid), bf16),
            pltpu.VMEM((nb * half, depth), bf16),
            pltpu.VMEM((2 * hid, 2 * cols), bf16),
            pltpu.VMEM((parts * nb, size, 4 * hid), bf16),
            pltpu.VMEM((parts * nb, size, 4 * hid), bf16),
            pltpu.VMEM((parts, size, 2 * hid), bf16),
            pltpu.VMEM((nz * half, 2 * hid), bf16),
            pltpu.VMEM((nz * half, 2 * cols), bf16),
        ] + [pltpu.SemaphoreType.DMA((n,)) for n in sems],
        compiler_params=pltpu.CompilerParams(
            collective_id=0, has_side_effects=True, vmem_limit_bytes=60 * 2**20
        ),
    )(tokens, gate_weight, up_weight, down_weight)


def solution(mesh):
    nb = mesh.shape["batch"]
    small = mesh.shape["mp"] == 2 and nb % 4 == 0
    return jax.shard_map(
        functools.partial(exchanged, nb) if small else gathered,
        mesh=mesh,
        in_specs=(
            P(("groups", "batch"), None),
            P("batch", "mp"),
            P("batch", "mp"),
            P("mp", "batch"),
        ),
        out_specs=P(("groups", "batch"), "mp"),
        check_vma=False,
    )
```
